32 devices in a mesh: fsdp: 4 (over x, core), ctx: 2 (over y), tp: 4 (over z).
Axes of the slice: x: 2, y: 2, z: 4, core: 2. Of those that a mesh axis runs over, the one named last changes fastest.
Arguments:
- latents: bfloat16 [4, 2048, 1152], P('fsdp', 'ctx'), may hold values from -6 to 6
- conditioning: bfloat16 [4, 1152], P('fsdp', 'tp'), may hold values from -6 to 6
- modulation_weight: bfloat16 [1152, 6, 1152], P('tp', None, ('fsdp', 'ctx')), may hold values from -0.1875 to 0.1875
- attention_weight: bfloat16 [1152, 3, 1152], P(('fsdp', 'ctx'), None, 'tp'), may hold values from -0.1875 to 0.1875
- output_weight: bfloat16 [1152, 1152], P('tp', ('fsdp', 'ctx')), may hold values from -3 to 3
- expand_weight: bfloat16 [1152, 4608], P(('fsdp', 'ctx'), 'tp'), may hold values from -0.1875 to 0.1875
- contract_weight: bfloat16 [4608, 1152], P('tp', ('fsdp', 'ctx')), may hold values from -0.09375 to 0.09375
- cotangent: bfloat16 [4, 2048, 1152], P('fsdp', 'ctx'), may hold values from -6 to 6
Outputs:
- block_out: bfloat16 [4, 2048, 1152], P('fsdp', 'ctx')
- latents_grad: bfloat16 [4, 2048, 1152], P('fsdp', 'ctx')
- conditioning_grad: float32 [4, 1152], P('fsdp', 'tp')
- modulation_grad: float32 [1152, 6, 1152], P('tp', None, ('fsdp', 'ctx'))
- attention_grad: float32 [1152, 3, 1152], P(('fsdp', 'ctx'), None, 'tp')
- output_grad: float32 [1152, 1152], P('tp', ('fsdp', 'ctx'))
- expand_grad: float32 [1152, 4608], P(('fsdp', 'ctx'), 'tp')
- contract_grad: float32 [4608, 1152], P('tp', ('fsdp', 'ctx'))
The draws below stay inside these ranges and needn't reach their ends.
All inputs are finite; a program needn't handle non-finite values.
Results may differ from the reference program's by a relative error of at most 0.014.
The reference program's roundings to bfloat16 on the way count: a program that leaves them out, or rounds other values in their place, can miss the bound.
Values may be sent and summed in bfloat16 or wider, within the bound.
A program may use at most 192 MiB of HBM per device.

```python
import jax
import jax.numpy as jnp
from jax import lax

D = 1152
HEADS = 16
HEAD_SIZE = 72
FF = 4608
SEQ = 2048
LATENTS = 4


def levels(key, extent, split, low, largest):
    factor_of = 1.0
    for position, parts in split:
        steps = jax.random.uniform(jax.random.fold_in(jax.random.fold_in(key, 6), position), (parts,), jnp.float32, low / len(split), largest / len(split))
        factor_of = factor_of * jnp.repeat(jnp.exp(steps), extent[position] // parts).reshape((-1,) + (1,) * (len(extent) - 1 - position))
    return factor_of


def normal_values(key, shape, deviation, most, shards=(), held_as=jnp.bfloat16):
    entries = deviation * jax.random.normal(key, shape, jnp.float32)
    if shards:
        entries = entries * levels(key, shape, shards, -0.22, 0.18)
    return jnp.clip(entries, -most, most).astype(held_as)


def setup_inputs(seed: int = 0) -> dict:
    key_of = jax.random.split(jax.random.key(seed), 9)
    latents = normal_values(key_of[0], (LATENTS, SEQ, D), 1.0, 6.0, ((0, 4), (1, 2)))
    conditioning = normal_values(key_of[1], (LATENTS, D), 1.0, 6.0, ((0, 4), (1, 4)))
    modulation_weight = normal_values(key_of[2], (D, 6, D), D ** -0.5, 0.1875, ((0, 4), (2, 8)))
    attention_weight = normal_values(key_of[3], (D, 3, D), D ** -0.5, 0.1875, ((0, 8), (2, 4)))
    output_weight = normal_values(key_of[4], (D, D), (max(8 * D // SEQ, 1)) ** -0.5, 3.0, ((0, 4), (1, 8)))
    expand_weight = normal_values(key_of[5], (D, FF), D ** -0.5, 0.1875, ((0, 8), (1, 4)))
    contract_weight = normal_values(key_of[6], (FF, D), FF ** -0.5, 0.09375, ((0, 4), (1, 8)))
    cotangent = normal_values(key_of[7], (LATENTS, SEQ, D), 1.0, 6.0, ((0, 4), (1, 2)))
    return {"latents": latents, "conditioning": conditioning, "modulation_weight": modulation_weight, "attention_weight": attention_weight, "output_weight": output_weight, "expand_weight": expand_weight, "contract_weight": contract_weight, "cotangent": cotangent}


highest = lax.Precision.HIGHEST
epsilon = 1e-06

@jax.custom_vjp
def low(v):
    return lax.optimization_barrier(v.astype(jnp.bfloat16)).astype(jnp.float32)

@jax.custom_vjp
def low_back(v):
    return v

def low_keep(v):
    return (low(v), None)

def low_pass(kept, grad):
    return (grad,)

def back_keep(v):
    return (v, None)

def back_low(kept, grad):
    return (low(grad),)
low.defvjp(low_keep, low_pass)
low_back.defvjp(back_keep, back_low)

def layer_norm(value_rows):
    centred = value_rows - lax.optimization_barrier(jnp.mean(value_rows, axis=-1, keepdims=True))
    spread = lax.optimization_barrier(jnp.mean(centred * centred, axis=-1, keepdims=True))
    return centred * lax.rsqrt(spread + epsilon)

def attend_block(queries, key_rows, value_rows):
    logit_scores = low_back(jnp.einsum('qhd,khd->hqk', queries, key_rows, precision=highest) * HEAD_SIZE ** (-0.5))
    top = lax.optimization_barrier(jnp.max(logit_scores, axis=-1, keepdims=True))
    expo = jnp.exp(logit_scores - top)
    probabilities = expo / lax.optimization_barrier(jnp.sum(expo, axis=-1, keepdims=True))
    return jnp.einsum('hqk,khd->qhd', low(probabilities), value_rows, precision=highest)

def block_one(tokens, cond_row, weights):
    modulation_w, attention_w, output_w, expand_w, contract_w = weights
    cond_act = low(jax.nn.silu(cond_row))
    modulations = jnp.einsum('d,dkc->kc', cond_act, modulation_w, precision=highest)
    act_one = low(layer_norm(tokens) * (1.0 + modulations[1]) + modulations[0])
    projected = low_back(low(jnp.einsum('td,dkc->tkc', act_one, attention_w, precision=highest)))
    queries = projected[:, 0].reshape(SEQ, HEADS, HEAD_SIZE)
    key_rows = projected[:, 1].reshape(SEQ, HEADS, HEAD_SIZE)
    value_rows = projected[:, 2].reshape(SEQ, HEADS, HEAD_SIZE)
    block_rows = min(512, SEQ)

    def one_block(query_rows):
        return attend_block(query_rows, key_rows, value_rows)
    mixed_values = lax.map(jax.checkpoint(one_block), queries.reshape(SEQ // block_rows, block_rows, HEADS, HEAD_SIZE))
    attended = low_back(low(mixed_values.reshape(SEQ, D)))
    branch_one = low_back(jnp.dot(attended, output_w, precision=highest))
    hidden = tokens + modulations[2] * branch_one
    act_two = low(layer_norm(hidden) * (1.0 + modulations[4]) + modulations[3])
    pre_gelu = low_back(jnp.dot(act_two, expand_w, precision=highest))
    activated = low(jax.nn.gelu(pre_gelu, approximate=True))
    branch_two = low_back(jnp.dot(activated, contract_w, precision=highest))
    return hidden + modulations[5] * branch_two

def forward(tokens, conditioning, weights):

    def one_latent(paired):
        return block_one(paired[0], paired[1], weights)
    return lax.map(jax.checkpoint(one_latent), (tokens, conditioning))

def reference(latents, conditioning, modulation_weight, attention_weight, output_weight, expand_weight, contract_weight, cotangent):
    weights = tuple((matrix.astype(jnp.float32) for matrix in (modulation_weight, attention_weight, output_weight, expand_weight, contract_weight)))
    block_out, pullback = jax.vjp(forward, latents.astype(jnp.float32), conditioning.astype(jnp.float32), weights)
    grad_tokens, grad_cond, grad_weights = pullback(cotangent.astype(jnp.float32))
    return (block_out.astype(jnp.bfloat16), grad_tokens.astype(jnp.bfloat16), grad_cond, grad_weights[0], grad_weights[1], grad_weights[2], grad_weights[3], grad_weights[4])
```

```python
from functools import partial

import jax
import jax.numpy as jnp
from jax import lax
from jax.sharding import PartitionSpec as P

HEAD_SIZE = 72


highest = lax.Precision.HIGHEST
epsilon = 1e-06


def layer_norm(value_rows):
    centred = value_rows - jnp.mean(value_rows, axis=-1, keepdims=True)
    spread = jnp.mean(centred * centred, axis=-1, keepdims=True)
    return centred * lax.rsqrt(spread + epsilon)


def modulate(value_rows, shift, scale):
    return layer_norm(value_rows) * (1.0 + scale[:, None, :]) + shift[:, None, :]


def head_major(value_rows):
    latent_count, row_count, width = value_rows.shape
    return value_rows.reshape(latent_count, row_count, width // HEAD_SIZE, HEAD_SIZE).transpose(
        2, 0, 1, 3
    )


def token_major(value_rows):
    head_count, latent_count, row_count, size = value_rows.shape
    return value_rows.transpose(1, 2, 0, 3).reshape(latent_count, row_count, head_count * size)


def forward_head(operands):
    query_matrix, key_rows, value_rows = operands
    logit_scores = jnp.einsum(
        "jxf,jrf->jxr", query_matrix, key_rows, preferred_element_type=jnp.float32
    ) * HEAD_SIZE ** (-0.5)
    top = jnp.max(logit_scores, axis=-1, keepdims=True)
    expo = jnp.exp(logit_scores - top)
    total = jnp.sum(expo, axis=-1, keepdims=True)
    probabilities = (expo / total).astype(jnp.bfloat16)
    mixed_values = jnp.einsum(
        "cms,csh->cmh", probabilities, value_rows, preferred_element_type=jnp.float32
    )
    return (mixed_values, (top + jnp.log(total))[..., 0])


def backward_head(operands):
    query_matrix, key_rows, value_rows, grad_mixed_rows, logsum = operands
    logit_scores = jnp.einsum(
        "jxf,jrf->jxr", query_matrix, key_rows, preferred_element_type=jnp.float32
    ) * HEAD_SIZE ** (-0.5)
    probabilities = jnp.exp(logit_scores - logsum[..., None])
    grad_probabilities = jnp.einsum(
        "jxf,jrf->jxr", grad_mixed_rows, value_rows, preferred_element_type=jnp.float32
    )
    inner = jnp.sum(probabilities * grad_probabilities, axis=-1, keepdims=True)
    grad_logit_scores = (probabilities * (grad_probabilities - inner)).astype(jnp.bfloat16)
    grad_query = jnp.einsum(
        "cms,csh->cmh", grad_logit_scores, key_rows, preferred_element_type=jnp.float32
    ) * HEAD_SIZE ** (-0.5)
    grad_keys = jnp.einsum(
        "vft,vfm->vtm", grad_logit_scores, query_matrix, preferred_element_type=jnp.float32
    ) * HEAD_SIZE ** (-0.5)
    grad_values = jnp.einsum(
        "vft,vfm->vtm",
        probabilities.astype(jnp.bfloat16),
        grad_mixed_rows,
        preferred_element_type=jnp.float32,
    )
    return (grad_query, grad_keys, grad_values)


def shards(
    latents,
    conditioning,
    modulation_weight,
    attention_weight,
    output_weight,
    expand_weight,
    contract_weight,
    cotangent,
):
    everywhere = ("fsdp", "ctx")
    qkv_full = lax.all_gather(attention_weight, everywhere, axis=0, tiled=True)
    ff_part = expand_weight.shape[1]
    rest = jnp.concatenate((output_weight.T, expand_weight, contract_weight.T), axis=1)
    rest_full = lax.all_gather(rest, everywhere, axis=0, tiled=True)
    head_part = output_weight.shape[0]
    out_t = rest_full[:, :head_part]
    expand_full = rest_full[:, head_part : head_part + ff_part]
    contract_t = rest_full[:, head_part + ff_part :]
    own_latent = lax.axis_index("fsdp")
    share_rows = latents.shape[1] // lax.axis_size("tp")
    share_start = lax.axis_index("tp") * share_rows
    cond_float = conditioning.astype(jnp.float32)
    cond_silu, silu_pull = jax.vjp(jax.nn.silu, cond_float)
    cond_act = cond_silu.astype(jnp.bfloat16)
    cond_all = lax.all_gather(cond_act, "fsdp", axis=0, tiled=True)
    mod_terms = jnp.einsum(
        "bd,dkc->bkc", cond_all, modulation_weight, preferred_element_type=jnp.float32
    )
    mod_parts = lax.all_gather(mod_terms, ("tp", "fsdp", "ctx"), axis=0)
    mod_parts = lax.dynamic_slice_in_dim(mod_parts, own_latent, 1, 1)
    column_parts = mod_parts.shape[0] // lax.axis_size("tp")
    mod_parts = mod_parts.reshape((lax.axis_size("tp"), column_parts) + mod_parts.shape[2:])
    modulations = jnp.sum(mod_parts, axis=0).transpose(1, 0, 2)
    modulations = modulations.reshape(1, modulations.shape[0], -1)
    shift_one = modulations[:, 0]
    scale_one = modulations[:, 1]
    gate_one = modulations[:, 2]
    shift_two = modulations[:, 3]
    scale_two = modulations[:, 4]
    gate_two = modulations[:, 5]
    tokens_float = latents.astype(jnp.float32)
    token_share = lax.dynamic_slice_in_dim(tokens_float, share_start, share_rows, 1)
    act_one = modulate(tokens_float, shift_one, scale_one).astype(jnp.bfloat16)
    projected = jnp.einsum(
        "btd,dkc->btkc", act_one, qkv_full, preferred_element_type=jnp.float32
    ).astype(jnp.bfloat16)
    pair_local = projected[:, :, 1:]
    pair_all = lax.all_gather(pair_local, "ctx", axis=1, tiled=True)
    heads_query = head_major(projected[:, :, 0])
    keys_heads = head_major(pair_all[:, :, 0])
    values_heads = head_major(pair_all[:, :, 1])
    mixed_values, logsum = lax.map(forward_head, (heads_query, keys_heads, values_heads))
    attended = token_major(mixed_values).astype(jnp.bfloat16)
    branch_one = lax.psum_scatter(
        jnp.einsum(
            "btc,dc->btd", attended, out_t, preferred_element_type=jnp.float32
        ).astype(jnp.bfloat16),
        "tp",
        scatter_dimension=1,
        tiled=True,
    ).astype(jnp.float32)
    hidden = token_share + gate_one[:, None, :] * branch_one
    normed_two, norm_pull_two = jax.vjp(modulate, hidden, shift_two, scale_two)
    act_two = lax.all_gather(normed_two.astype(jnp.bfloat16), "tp", axis=1, tiled=True)
    pre_gelu = jnp.einsum("btd,df->btf", act_two, expand_full, preferred_element_type=jnp.float32)
    gelu_value, gelu_pull = jax.vjp(partial(jax.nn.gelu, approximate=True), pre_gelu)
    activated = gelu_value.astype(jnp.bfloat16)
    branch_two = lax.psum_scatter(
        jnp.einsum(
            "btf,df->btd", activated, contract_t, preferred_element_type=jnp.float32
        ).astype(jnp.bfloat16),
        "tp",
        scatter_dimension=1,
        tiled=True,
    ).astype(jnp.float32)
    block_share = (hidden + gate_two[:, None, :] * branch_two).astype(jnp.bfloat16)
    grad_out_full = cotangent.astype(jnp.float32)
    grad_out = lax.dynamic_slice_in_dim(grad_out_full, share_start, share_rows, 1)
    grad_gate_two = jnp.sum(grad_out * branch_two, axis=1)
    grad_branch_two = (grad_out_full * gate_two[:, None, :]).astype(jnp.bfloat16)
    grad_activated = jnp.einsum(
        "btd,df->btf", grad_branch_two, contract_t, preferred_element_type=jnp.float32
    )
    grad_pre = gelu_pull(grad_activated)[0].astype(jnp.bfloat16)
    grad_contract = jnp.einsum(
        "btd,btf->df", grad_branch_two, activated, preferred_element_type=jnp.float32
    )
    grad_act_two = lax.psum_scatter(
        jnp.einsum(
            "btf,df->btd", grad_pre, expand_full, preferred_element_type=jnp.float32
        ).astype(jnp.bfloat16),
        "tp",
        scatter_dimension=1,
        tiled=True,
    ).astype(jnp.float32)
    grad_expand = jnp.einsum("btd,btf->df", act_two, grad_pre, preferred_element_type=jnp.float32)
    grad_hidden, grad_shift_two, grad_scale_two = norm_pull_two(grad_act_two)
    grad_hidden = grad_hidden + grad_out
    grad_gate_one = jnp.sum(grad_hidden * branch_one, axis=1)
    branch_grad_share = (grad_hidden * gate_one[:, None, :]).astype(jnp.bfloat16)
    grad_branch_one = lax.all_gather(branch_grad_share, "tp", axis=1, tiled=True)
    grad_attended = jnp.einsum(
        "btd,dc->btc", grad_branch_one, out_t, preferred_element_type=jnp.float32
    ).astype(jnp.bfloat16)
    grad_output = jnp.einsum(
        "btd,btc->dc", grad_branch_one, attended, preferred_element_type=jnp.float32
    )
    grad_rest = jnp.concatenate((grad_output, grad_expand, grad_contract), axis=1)
    grad_rest = lax.psum_scatter(
        grad_rest.astype(jnp.bfloat16), everywhere, scatter_dimension=0, tiled=True
    ).astype(jnp.float32)
    heads_grad = head_major(grad_attended)
    grads_query, grads_keys, grads_values = lax.map(
        backward_head, (heads_query, keys_heads, values_heads, heads_grad, logsum)
    )
    pair_terms = jnp.stack((token_major(grads_keys), token_major(grads_values)), axis=2)
    pair_terms = pair_terms.astype(jnp.bfloat16)
    grad_pair = lax.psum_scatter(pair_terms, "ctx", scatter_dimension=1, tiled=True).astype(
        jnp.bfloat16
    )
    grad_query = token_major(grads_query).astype(jnp.bfloat16)
    grad_projected = jnp.concatenate((grad_query[:, :, None], grad_pair), axis=2)
    grad_act_one = lax.psum_scatter(
        jnp.einsum(
            "btkc,dkc->btd", grad_projected, qkv_full, preferred_element_type=jnp.float32
        ).astype(jnp.bfloat16),
        "tp",
        scatter_dimension=1,
        tiled=True,
    ).astype(jnp.float32)
    grad_attention = jnp.einsum(
        "btd,btkc->dkc", act_one, grad_projected, preferred_element_type=jnp.float32
    )
    normed_share, norm_pull_one = jax.vjp(modulate, token_share, shift_one, scale_one)
    grad_tokens, grad_shift_one, grad_scale_one = norm_pull_one(grad_act_one)
    grad_tokens = grad_tokens + grad_hidden
    block_out, latents_grad = (
        lax.all_gather(block_share, "tp", axis=1, tiled=True),
        lax.all_gather(grad_tokens.astype(jnp.bfloat16), "tp", axis=1, tiled=True),
    )
    grad_parts = jnp.stack(
        (
            grad_shift_one,
            grad_scale_one,
            grad_gate_one,
            grad_shift_two,
            grad_scale_two,
            grad_gate_two,
        ),
        axis=1,
    )
    grad_attention = lax.psum_scatter(
        grad_attention.astype(jnp.bfloat16), everywhere, scatter_dimension=0, tiled=True
    ).astype(jnp.float32)
    grad_modulations = lax.all_gather(grad_parts[0], ("ctx", "tp", "fsdp"), axis=0)
    latent_count = lax.axis_size("fsdp")
    grad_modulations = jnp.sum(
        grad_modulations.reshape((-1, latent_count) + grad_modulations.shape[1:]), axis=0
    )
    column_count = modulation_weight.shape[2]
    column_start = lax.axis_index(everywhere) * column_count
    grad_columns = lax.dynamic_slice_in_dim(grad_modulations, column_start, column_count, 2)
    grad_modulation = jnp.einsum(
        "bd,bkc->dkc", cond_all.astype(jnp.float32), grad_columns, precision=highest
    )
    grad_cond_terms = jnp.einsum(
        "bkc,dkc->bd", grad_columns, modulation_weight.astype(jnp.float32), precision=highest
    )
    grad_cond_act = lax.dynamic_slice_in_dim(
        lax.psum(grad_cond_terms, everywhere), own_latent, 1, 0
    )
    conditioning_grad = silu_pull(grad_cond_act)[0]
    return (
        block_out,
        latents_grad,
        conditioning_grad,
        grad_modulation,
        grad_attention,
        grad_rest[:, :head_part].T,
        grad_rest[:, head_part : head_part + ff_part],
        grad_rest[:, head_part + ff_part :].T,
    )


def solution(mesh):
    return jax.shard_map(
        shards,
        mesh=mesh,
        in_specs=(
            P("fsdp", "ctx", None),
            P("fsdp", "tp"),
            P("tp", None, ("fsdp", "ctx")),
            P(("fsdp", "ctx"), None, "tp"),
            P("tp", ("fsdp", "ctx")),
            P(("fsdp", "ctx"), "tp"),
            P("tp", ("fsdp", "ctx")),
            P("fsdp", "ctx", None),
        ),
        out_specs=(
            P("fsdp", "ctx", None),
            P("fsdp", "ctx", None),
            P("fsdp", "tp"),
            P("tp", None, ("fsdp", "ctx")),
            P(("fsdp", "ctx"), None, "tp"),
            P("tp", ("fsdp", "ctx")),
            P(("fsdp", "ctx"), "tp"),
            P("tp", ("fsdp", "ctx")),
        ),
        check_vma=False,
    )
```

```python
from functools import partial

import jax
import jax.numpy as jnp
from jax import lax
from jax.sharding import PartitionSpec as P

HEAD_SIZE = 72


highest = lax.Precision.HIGHEST
epsilon = 1e-06


def layer_norm(value_rows):
    centred = value_rows - jnp.mean(value_rows, axis=-1, keepdims=True)
    spread = jnp.mean(centred * centred, axis=-1, keepdims=True)
    return centred * lax.rsqrt(spread + epsilon)


def modulate(value_rows, shift, scale):
    return layer_norm(value_rows) * (1.0 + scale[:, None, :]) + shift[:, None, :]


def head_major(value_rows):
    latent_count, row_count, width = value_rows.shape
    return value_rows.reshape(latent_count, row_count, width // HEAD_SIZE, HEAD_SIZE).transpose(
        2, 0, 1, 3
    )


def token_major(value_rows):
    head_count, latent_count, row_count, size = value_rows.shape
    return value_rows.transpose(1, 2, 0, 3).reshape(latent_count, row_count, head_count * size)


def shifted(block, axis_name, step):
    size = lax.axis_size(axis_name)
    return lax.ppermute(block, axis_name, [(i, (i + step) % size) for i in range(size)])


def gather_rows(block, axis_name):
    size = lax.axis_size(axis_name)
    position = lax.axis_index(axis_name)
    rows = block.shape[1]
    whole = jnp.zeros(block.shape[:1] + (size * rows,) + block.shape[2:], block.dtype)
    whole = lax.dynamic_update_slice_in_dim(whole, block, position * rows, 1)
    for step in range(1, size):
        source = lax.rem(position - step + size, size)
        whole = lax.dynamic_update_slice_in_dim(
            whole, shifted(block, axis_name, step), source * rows, 1
        )
    return whole


def scatter_sum(terms, axis_name):
    size = lax.axis_size(axis_name)
    position = lax.axis_index(axis_name)
    rows = terms.shape[1] // size
    total = lax.dynamic_slice_in_dim(terms, position * rows, rows, 1).astype(jnp.float32)
    for step in range(1, size):
        target = lax.rem(position + step, size)
        part = lax.dynamic_slice_in_dim(terms, target * rows, rows, 1).astype(jnp.bfloat16)
        total = total + shifted(part, axis_name, step).astype(jnp.float32)
    return total


def forward_head(operands):
    query_matrix, key_rows, value_rows = operands
    logit_scores = jnp.einsum(
        "jxf,jrf->jxr", query_matrix, key_rows, preferred_element_type=jnp.float32
    ) * HEAD_SIZE ** (-0.5)
    top = jnp.max(logit_scores, axis=-1, keepdims=True)
    expo = jnp.exp(logit_scores - top)
    total = jnp.sum(expo, axis=-1, keepdims=True)
    probabilities = (expo / total).astype(jnp.bfloat16)
    mixed_values = jnp.einsum(
        "cms,csh->cmh", probabilities, value_rows, preferred_element_type=jnp.float32
    )
    return (mixed_values, (top + jnp.log(total))[..., 0])


def backward_head(operands):
    query_matrix, key_rows, value_rows, grad_mixed_rows, logsum = operands
    logit_scores = jnp.einsum(
        "jxf,jrf->jxr", query_matrix, key_rows, preferred_element_type=jnp.float32
    ) * HEAD_SIZE ** (-0.5)
    probabilities = jnp.exp(logit_scores - logsum[..., None])
    grad_probabilities = jnp.einsum(
        "jxf,jrf->jxr", grad_mixed_rows, value_rows, preferred_element_type=jnp.float32
    )
    inner = jnp.sum(probabilities * grad_probabilities, axis=-1, keepdims=True)
    grad_logit_scores = (probabilities * (grad_probabilities - inner)).astype(jnp.bfloat16)
    grad_query = jnp.einsum(
        "cms,csh->cmh", grad_logit_scores, key_rows, preferred_element_type=jnp.float32
    ) * HEAD_SIZE ** (-0.5)
    grad_keys = jnp.einsum(
        "vft,vfm->vtm", grad_logit_scores, query_matrix, preferred_element_type=jnp.float32
    ) * HEAD_SIZE ** (-0.5)
    grad_values = jnp.einsum(
        "vft,vfm->vtm",
        probabilities.astype(jnp.bfloat16),
        grad_mixed_rows,
        preferred_element_type=jnp.float32,
    )
    return (grad_query, grad_keys, grad_values)


def shards(
    latents,
    conditioning,
    modulation_weight,
    attention_weight,
    output_weight,
    expand_weight,
    contract_weight,
    cotangent,
):
    everywhere = ("fsdp", "ctx")
    qkv_full = lax.all_gather(attention_weight, everywhere, axis=0, tiled=True)
    ff_part = expand_weight.shape[1]
    rest = jnp.concatenate((output_weight.T, expand_weight, contract_weight.T), axis=1)
    rest_full = lax.all_gather(rest, everywhere, axis=0, tiled=True)
    head_part = output_weight.shape[0]
    out_t = rest_full[:, :head_part]
    expand_full = rest_full[:, head_part : head_part + ff_part]
    contract_t = rest_full[:, head_part + ff_part :]
    own_latent = lax.axis_index("fsdp")
    share_rows = latents.shape[1] // lax.axis_size("tp")
    share_start = lax.axis_index("tp") * share_rows
    cond_float = conditioning.astype(jnp.float32)
    cond_silu, silu_pull = jax.vjp(jax.nn.silu, cond_float)
    cond_act = cond_silu.astype(jnp.bfloat16)
    cond_all = lax.all_gather(cond_act, "fsdp", axis=0, tiled=True)
    mod_terms = jnp.einsum(
        "bd,dkc->bkc", cond_all, modulation_weight, preferred_element_type=jnp.float32
    )
    vector_count, part_columns = mod_terms.shape[1:]
    mod_terms = mod_terms.reshape(mod_terms.shape[0], -1)
    mod_parts = jnp.sum(lax.all_gather(mod_terms, "tp", axis=0), axis=0)
    mod_parts = lax.all_gather(lax.all_gather(mod_parts, "ctx", axis=0), "fsdp", axis=0)
    mod_parts = lax.dynamic_slice_in_dim(mod_parts, own_latent, 1, 2)
    mod_parts = mod_parts.reshape(-1, vector_count, part_columns)
    modulations = mod_parts.transpose(1, 0, 2).reshape(1, vector_count, -1)
    shift_one = modulations[:, 0]
    scale_one = modulations[:, 1]
    gate_one = modulations[:, 2]
    shift_two = modulations[:, 3]
    scale_two = modulations[:, 4]
    gate_two = modulations[:, 5]
    tokens_float = latents.astype(jnp.float32)
    token_share = lax.dynamic_slice_in_dim(tokens_float, share_start, share_rows, 1)
    act_one = modulate(tokens_float, shift_one, scale_one).astype(jnp.bfloat16)
    projected = jnp.einsum(
        "btd,dkc->btkc", act_one, qkv_full, preferred_element_type=jnp.float32
    ).astype(jnp.bfloat16)
    pair_local = projected[:, :, 1:]
    pair_all = gather_rows(pair_local, "ctx")
    heads_query = head_major(projected[:, :, 0])
    keys_heads = head_major(pair_all[:, :, 0])
    values_heads = head_major(pair_all[:, :, 1])
    mixed_values, logsum = lax.map(forward_head, (heads_query, keys_heads, values_heads))
    attended = token_major(mixed_values).astype(jnp.bfloat16)
    branch_one = scatter_sum(
        jnp.einsum("btc,dc->btd", attended, out_t, preferred_element_type=jnp.float32), "tp"
    )
    hidden = token_share + gate_one[:, None, :] * branch_one
    normed_two, norm_pull_two = jax.vjp(modulate, hidden, shift_two, scale_two)
    act_two = gather_rows(normed_two.astype(jnp.bfloat16), "tp")
    pre_gelu = jnp.einsum("btd,df->btf", act_two, expand_full, preferred_element_type=jnp.float32)
    gelu_value, gelu_pull = jax.vjp(partial(jax.nn.gelu, approximate=True), pre_gelu)
    activated = gelu_value.astype(jnp.bfloat16)
    branch_two_terms = jnp.einsum(
        "btf,df->btd", activated, contract_t, preferred_element_type=jnp.float32
    ).astype(jnp.bfloat16)
    grad_out_full = cotangent.astype(jnp.float32)
    grad_out = lax.dynamic_slice_in_dim(grad_out_full, share_start, share_rows, 1)
    grad_branch_two = (grad_out_full * gate_two[:, None, :]).astype(jnp.bfloat16)
    grad_activated = jnp.einsum(
        "btd,df->btf", grad_branch_two, contract_t, preferred_element_type=jnp.float32
    )
    grad_pre = gelu_pull(grad_activated)[0].astype(jnp.bfloat16)
    grad_contract = jnp.einsum(
        "btd,btf->df", grad_branch_two, activated, preferred_element_type=jnp.float32
    )
    grad_act_two = scatter_sum(
        jnp.einsum("btf,df->btd", grad_pre, expand_full, preferred_element_type=jnp.float32),
        "tp",
    )
    grad_expand = jnp.einsum("btd,btf->df", act_two, grad_pre, preferred_element_type=jnp.float32)
    grad_hidden, grad_shift_two, grad_scale_two = norm_pull_two(grad_act_two)
    grad_hidden = grad_hidden + grad_out
    grad_gate_one = jnp.sum(grad_hidden * branch_one, axis=1)
    branch_grad_share = (grad_hidden * gate_one[:, None, :]).astype(jnp.bfloat16)
    grad_branch_one = gather_rows(branch_grad_share, "tp")
    grad_branch_one, branch_two_terms, grad_expand, grad_contract = lax.optimization_barrier(
        (
            grad_branch_one,
            branch_two_terms,
            grad_expand.astype(jnp.bfloat16),
            grad_contract.astype(jnp.bfloat16),
        )
    )
    branch_two = scatter_sum(branch_two_terms, "tp")
    grad_attended = jnp.einsum(
        "btd,dc->btc", grad_branch_one, out_t, preferred_element_type=jnp.float32
    ).astype(jnp.bfloat16)
    grad_output = jnp.einsum(
        "btd,btc->dc", grad_branch_one, attended, preferred_element_type=jnp.float32
    )
    grad_rest = jnp.concatenate(
        (grad_output.astype(jnp.bfloat16), grad_expand, grad_contract), axis=1
    )
    grad_rest, grad_attended = lax.optimization_barrier((grad_rest, grad_attended))
    grad_rest = lax.psum_scatter(grad_rest, everywhere, scatter_dimension=0, tiled=True)
    heads_grad = head_major(grad_attended)
    per_head = []
    head_inputs = (heads_query, keys_heads, values_heads, heads_grad, logsum)
    head_count = heads_query.shape[0]
    for head in range(head_count):
        operands = tuple(array[head] for array in head_inputs)
        if head == max(head_count // 2, 1):
            operands, per_head[-1], branch_two = lax.optimization_barrier(
                (operands, per_head[-1], branch_two)
            )
        elif head > 0:
            operands, per_head[-1] = lax.optimization_barrier((operands, per_head[-1]))
        per_head.append(backward_head(operands))
    block_share = (hidden + gate_two[:, None, :] * branch_two).astype(jnp.bfloat16)
    grad_gate_two = jnp.sum(grad_out * branch_two, axis=1)
    block_out = gather_rows(block_share, "tp")
    per_head[-1], block_out, grad_rest = lax.optimization_barrier(
        (per_head[-1], block_out, grad_rest)
    )
    grads_query, grads_keys, grads_values = (jnp.stack(parts) for parts in zip(*per_head))
    pair_terms = jnp.stack((token_major(grads_keys), token_major(grads_values)), axis=2)
    grad_pair = scatter_sum(pair_terms, "ctx").astype(jnp.bfloat16)
    grad_query = token_major(grads_query).astype(jnp.bfloat16)
    grad_projected = jnp.concatenate((grad_query[:, :, None], grad_pair), axis=2)
    grad_act_one = scatter_sum(
        jnp.einsum(
            "btkc,dkc->btd", grad_projected, qkv_full, preferred_element_type=jnp.float32
        ),
        "tp",
    )
    grad_rest = grad_rest.astype(jnp.float32)
    grad_attention = jnp.einsum(
        "btd,btkc->dkc", act_one, grad_projected, preferred_element_type=jnp.float32
    )
    grad_attention = lax.psum_scatter(
        grad_attention.astype(jnp.bfloat16), everywhere, scatter_dimension=0, tiled=True
    )
    grad_act_one, grad_attention = lax.optimization_barrier((grad_act_one, grad_attention))
    grad_attention = grad_attention.astype(jnp.float32)
    normed_share, norm_pull_one = jax.vjp(modulate, token_share, shift_one, scale_one)
    grad_tokens, grad_shift_one, grad_scale_one = norm_pull_one(grad_act_one)
    grad_tokens = grad_tokens + grad_hidden
    latents_grad = gather_rows(grad_tokens.astype(jnp.bfloat16), "tp")
    grad_parts = jnp.stack(
        (
            grad_shift_one,
            grad_scale_one,
            grad_gate_one,
            grad_shift_two,
            grad_scale_two,
            grad_gate_two,
        ),
        axis=1,
    )
    grad_parts = grad_parts.reshape(1, -1)
    grad_sums = jnp.sum(lax.all_gather(grad_parts, "tp", axis=0), axis=0)
    grad_sums = jnp.sum(lax.all_gather(grad_sums, "ctx", axis=0), axis=0)
    grad_modulations = lax.all_gather(grad_sums, "fsdp", axis=0, tiled=True)
    grad_modulations = grad_modulations.reshape(grad_modulations.shape[0], vector_count, -1)
    column_count = modulation_weight.shape[2]
    column_start = lax.axis_index(everywhere) * column_count
    grad_columns = lax.dynamic_slice_in_dim(grad_modulations, column_start, column_count, 2)
    grad_modulation = jnp.einsum(
        "bd,bkc->dkc", cond_all.astype(jnp.float32), grad_columns, precision=highest
    )
    grad_cond_terms = jnp.einsum(
        "bkc,dkc->bd", grad_columns, modulation_weight.astype(jnp.float32), precision=highest
    )
    grad_cond_act = lax.dynamic_slice_in_dim(
        lax.psum(grad_cond_terms, everywhere), own_latent, 1, 0
    )
    conditioning_grad = silu_pull(grad_cond_act)[0]
    return (
        block_out,
        latents_grad,
        conditioning_grad,
        grad_modulation,
        grad_attention,
        grad_rest[:, :head_part].T,
        grad_rest[:, head_part : head_part + ff_part],
        grad_rest[:, head_part + ff_part :].T,
    )


def solution(mesh):
    return jax.shard_map(
        shards,
        mesh=mesh,
        in_specs=(
            P("fsdp", "ctx", None),
            P("fsdp", "tp"),
            P("tp", None, ("fsdp", "ctx")),
            P(("fsdp", "ctx"), None, "tp"),
            P("tp", ("fsdp", "ctx")),
            P(("fsdp", "ctx"), "tp"),
            P("tp", ("fsdp", "ctx")),
            P("fsdp", "ctx", None),
        ),
        out_specs=(
            P("fsdp", "ctx", None),
            P("fsdp", "ctx", None),
            P("fsdp", "tp"),
            P("tp", None, ("fsdp", "ctx")),
            P(("fsdp", "ctx"), None, "tp"),
            P("tp", ("fsdp", "ctx")),
            P(("fsdp", "ctx"), "tp"),
            P("tp", ("fsdp", "ctx")),
        ),
        check_vma=False,
    )
```
